256 devices in a mesh: curve: 128 (over z, x, y), field: 2 (over core).
Axes of the slice: x: 4, y: 4, z: 8, core: 2. Of those that a mesh axis runs over, the one named last changes fastest.
Arguments:
- atm_flux: float32 [64, 524288], P('field', 'curve'), may hold values from 0.5 to 2
- ocean_state: float32 [64, 1048576], P('field', 'curve'), may hold values from 0.5 to 2
- area_atm: float32 [524288], P('curve'), may hold values from 0.5 to 18, as said below
- area_ocean: float32 [1048576], P('curve'), may hold values from 0.5 to 18, as said below
- tiles: float32 [16384, 128, 128], P('curve'), may hold values from 0 to 0.0078125
- tile_row: int32 [16384], P('curve'), may hold values from 0 to 8191, as said below
- tile_col: int32 [16384], P('curve'), may hold values from 0 to 4095, as said below
- tile_count: int32 [128], P('curve'), may hold values from 16 to 128, as said below
Outputs:
- ocean_flux: float32 [64, 1048576], P('field', 'curve')
- atm_fixed: float32 [64, 524288], P('field', 'curve')
The draws below stay inside these ranges and needn't reach their ends.
Inputs may be any that keep to these rules, and one draw needn't show every extreme that they name: `tile_row`: slots of device d name ocean blocks of that device, d * 64 to (d + 1) * 64 - 1. `tile_col`: slots of device d name atmosphere blocks within 16 blocks of that device's own blocks d * 32 to (d + 1) * 32 - 1, counted around the closed curve of 4096 blocks; the first slot of every device names d * 32 + 47 and the second d * 32 - 16, around the curve. `tile_count`: the live slots of a device are its first ones; the others are not part of the remap; some device has all 128 slots live. `area_atm`: positive. `area_ocean`: positive.
All inputs are finite; a program needn't handle non-finite values.
Results may differ from the reference program's by a relative error of at most 0.0003.
Values sent between devices are 32-bit elements; how exact they have to be, the bound alone decides.
A program may use at most 64 MiB of HBM per device.

```python
import jax
import jax.numpy as jnp
from jax import lax

FIELDS = 64
BLOCK = 128
AB_DEV = 32
TILE_CAP = 128
OB_DEV = 64
HALO = 16
ABLOCKS = 4096
OBLOCKS = 8192
ACELLS = 524288
OCELLS = 1048576
TILES_ALL = 16384
N_CURVE = 128


def area_law(key, cells):
    position = jnp.arange(cells, dtype=jnp.float32) / cells
    base = jnp.exp(jax.random.uniform(key, (cells,), jnp.float32, jnp.log(0.5), jnp.log(2.0)))
    rising = 1.0 + 2.0 * position
    return rising * base


def draw_area_atm(key, part):
    key = jax.random.fold_in(key, 5)
    return area_law(key, ACELLS)


def draw_area_ocean(key, part):
    key = jax.random.fold_in(key, 6)
    return area_law(key, OCELLS)


def draw_tile_row(key, part):
    key = jax.random.fold_in(key, 1)
    owner = jnp.arange(TILES_ALL, dtype=jnp.int32) // TILE_CAP
    return owner * OB_DEV + jax.random.randint(key, (TILES_ALL,), 0, OB_DEV, jnp.int32)


def draw_tile_col(key, part):
    key = jax.random.fold_in(key, 2)
    slot_index = jnp.arange(TILES_ALL, dtype=jnp.int32)
    owner = slot_index // TILE_CAP
    within = slot_index % TILE_CAP
    offset = jax.random.randint(key, (TILES_ALL,), -HALO, AB_DEV + HALO, jnp.int32)
    offset = jnp.where(within == 0, AB_DEV + HALO - 1, offset)
    offset = jnp.where(within == 1, -HALO, offset)
    return (owner * AB_DEV + offset) % ABLOCKS


def draw_tile_count(key, part):
    key = jax.random.fold_in(key, 3)
    first, second = jax.random.split(key)
    shifts = jax.random.randint(first, (N_CURVE,), 0, 4, jnp.int32)
    counts = jnp.right_shift(jnp.full((N_CURVE,), TILE_CAP, jnp.int32), shifts)
    fullest = jax.random.randint(second, (), 0, N_CURVE, jnp.int32)
    return jnp.where(jnp.arange(N_CURVE, dtype=jnp.int32) == fullest, TILE_CAP, counts)


def level_of(own_key, dims, cuts, least, top_value):
    factor_of, own = 1.0, jax.random.fold_in(own_key, 6)
    for dim, blocks in cuts:
        heights = jnp.exp(jax.random.uniform(jax.random.fold_in(own, dim), (blocks,), jnp.float32, least / len(cuts), top_value / len(cuts)))
        factor_of = factor_of * jnp.repeat(heights, dims[dim] // blocks).reshape([-1 if axis == dim else 1 for axis in range(len(dims))])
    return factor_of


def setup_inputs(seed: int = 0) -> dict:
    key_of = jax.random.split(jax.random.key(seed), 9)
    atm_flux = jnp.clip(0.5 + 1.5 * jax.random.uniform(key_of[0], (FIELDS, ACELLS), jnp.float32) ** level_of(key_of[0], (FIELDS, ACELLS), ((0, 2), (1, 128)), -0.2, 0.2), 0.5, 2.0)
    ocean_state = jnp.clip(0.5 + 1.5 * jax.random.uniform(key_of[1], (FIELDS, OCELLS), jnp.float32) ** level_of(key_of[1], (FIELDS, OCELLS), ((0, 2), (1, 128)), -0.2, 0.2), 0.5, 2.0)
    area_atm = draw_area_atm(jax.random.fold_in(key_of[8], 71), 0)
    area_ocean = draw_area_ocean(jax.random.fold_in(key_of[8], 71), 0)
    tiles = jnp.clip(0.0078125 * jax.random.uniform(key_of[4], (TILES_ALL, BLOCK, BLOCK), jnp.float32) ** level_of(key_of[4], (TILES_ALL, BLOCK, BLOCK), ((0, 128),), -0.2, 0.2), 0.0, 0.0078125)
    tile_row = draw_tile_row(jax.random.fold_in(key_of[8], 71), 0)
    tile_col = draw_tile_col(jax.random.fold_in(key_of[8], 71), 0)
    tile_count = draw_tile_count(jax.random.fold_in(key_of[8], 71), 0)
    return dict(atm_flux=atm_flux, ocean_state=ocean_state, area_atm=area_atm, area_ocean=area_ocean, tiles=tiles, tile_row=tile_row, tile_col=tile_col, tile_count=tile_count)


def reference(atm_flux, ocean_state, area_atm, area_ocean, tiles, tile_row, tile_col, tile_count):
    exact_mode = lax.Precision.HIGHEST
    atm_blocks = atm_flux.reshape(FIELDS, ABLOCKS, BLOCK)
    weighted = (ocean_state * area_ocean[None, :]).reshape(FIELDS, OBLOCKS, BLOCK)
    slot_index = jnp.arange(TILE_CAP, dtype=jnp.int32)
    window_span = AB_DEV + 2 * HALO

    def one_device(device):
        start = device * TILE_CAP
        weights = lax.dynamic_slice_in_dim(tiles, start, TILE_CAP, 0)
        slot_rows = lax.dynamic_slice_in_dim(tile_row, start, TILE_CAP, 0)
        slot_cols = lax.dynamic_slice_in_dim(tile_col, start, TILE_CAP, 0)
        live = (slot_index < tile_count[device]).astype(jnp.float32)
        forward = jnp.einsum("tij,ftj->tfi", weights, atm_blocks[:, slot_cols, :], precision=exact_mode)
        forward = forward * live[:, None, None]
        slab = jax.ops.segment_sum(forward, (slot_rows - device * OB_DEV).astype(jnp.int32), OB_DEV)
        backward = jnp.einsum("tij,fti->tfj", weights, weighted[:, slot_rows, :], precision=exact_mode)
        backward = backward * live[:, None, None]
        place = ((slot_cols - device * AB_DEV + HALO) % ABLOCKS).astype(jnp.int32)
        window = jax.ops.segment_sum(backward, place, window_span)
        return slab, window

    slabs, windows = lax.map(one_device, jnp.arange(N_CURVE, dtype=jnp.int32))
    ocean_remap = slabs.reshape(OBLOCKS, FIELDS, BLOCK).transpose(1, 0, 2).reshape(FIELDS, OCELLS)
    core = windows[:, HALO:HALO + AB_DEV]
    from_below = jnp.roll(windows[:, HALO + AB_DEV:], 1, axis=0)
    from_above = jnp.roll(windows[:, :HALO], -1, axis=0)
    core = core.at[:, :HALO].add(from_below)
    core = core.at[:, AB_DEV - HALO:].add(from_above)
    back_sum = core.reshape(ABLOCKS, FIELDS, BLOCK).transpose(1, 0, 2).reshape(FIELDS, ACELLS)
    target_ocean = jnp.sum(atm_flux * area_atm[None, :], axis=1)
    got_ocean = jnp.sum(ocean_remap * area_ocean[None, :], axis=1)
    ocean_flux = ocean_remap * (target_ocean / got_ocean)[:, None]
    target_atm = jnp.sum(ocean_state * area_ocean[None, :], axis=1)
    got_atm = jnp.sum(back_sum, axis=1)
    atm_fixed = back_sum / area_atm[None, :] * (target_atm / got_atm)[:, None]
    return ocean_flux, atm_fixed
```

```python
import functools

import jax
import jax.numpy as jnp
from jax import lax
from jax.experimental import pallas as pl
from jax.experimental.pallas import tpu as pltpu
from jax.sharding import PartitionSpec as P


def with_halo(block, sides, width):
    for axis, dim in sides:
        count = lax.axis_size(axis)
        forward = [(i, i + 1) for i in range(count - 1)]
        forward.append((count - 1, 0))
        backward = [(target, source) for source, target in forward]
        low = lax.ppermute(
            lax.slice_in_dim(block, block.shape[dim] - width, None, axis=dim), axis, forward
        )
        high = lax.ppermute(lax.slice_in_dim(block, 0, width, axis=dim), axis, backward)
        block = jnp.concatenate([low, block, high], axis=dim)
    return block


def from_behind(shard, axis, by):
    size = lax.axis_size(axis)
    return lax.ppermute(shard, axis, [(i, (i + by) % size) for i in range(size)])


def slot_terms(
    weights,
    slot_rows,
    slot_cols,
    live_slots,
    source_blocks,
    weighted_blocks,
    ocean_span,
    window_span,
):
    exact_mode = lax.Precision.HIGHEST
    forward = jnp.einsum(
        "tij,ftj->fti", weights, source_blocks[:, slot_cols, :], precision=exact_mode
    )
    row_onehot = (slot_rows[:, None] == jnp.arange(ocean_span, dtype=jnp.int32)[None, :]).astype(
        jnp.float32
    )
    row_onehot = row_onehot * live_slots[:, None]
    ocean_part = jnp.einsum("to,fti->foi", row_onehot, forward, precision=exact_mode)
    backward = jnp.einsum(
        "tij,fti->ftj", weights, weighted_blocks[:, slot_rows, :], precision=exact_mode
    )
    col_onehot = (slot_cols[:, None] == jnp.arange(window_span, dtype=jnp.int32)[None, :]).astype(
        jnp.float32
    )
    col_onehot = col_onehot * live_slots[:, None]
    window_part = jnp.einsum("tw,ftj->fwj", col_onehot, backward, precision=exact_mode)
    return (ocean_part, window_part)


PLANE = 16
MESH = pl.DeviceIdType.MESH


def sum_kernel(layers, mine, out, work, got_plane, got_line, send_plane, recv_plane, send_line, recv_line):
    me = lax.axis_index("curve")
    core = lax.axis_index("field")
    layer, place = me // PLANE, me % PLANE

    def plane_partner(k):
        return (layer * PLANE + (place + k) % PLANE, core)

    def line_partner(k):
        return ((layer + k) % layers * PLANE + place, core)

    barrier = pltpu.get_barrier_semaphore()
    for k in range(1, PLANE):
        pl.semaphore_signal(barrier, inc=1, device_id=plane_partner(k), device_id_type=MESH)
    for k in range(1, layers):
        pl.semaphore_signal(barrier, inc=1, device_id=line_partner(k), device_id_type=MESH)
    pl.semaphore_wait(barrier, PLANE + layers - 2)

    def exchange(source, count, partner, landed, send, recv):
        for k in range(1, count):
            pltpu.make_async_remote_copy(
                src_ref=source,
                dst_ref=landed.at[k - 1],
                send_sem=send,
                recv_sem=recv,
                device_id=partner(k),
                device_id_type=MESH,
            ).start()
        pltpu.make_async_copy(landed, landed, recv).wait()

    exchange(mine, PLANE, plane_partner, got_plane, send_plane, recv_plane)
    work[...] = mine[...] + jnp.sum(got_plane[...], axis=0)
    exchange(work, layers, line_partner, got_line, send_line, recv_line)
    out[...] = work[...] + jnp.sum(got_line[...], axis=0)
    pltpu.make_async_copy(got_plane, got_plane, send_plane).wait()
    pltpu.make_async_copy(got_line, got_line, send_line).wait()


def sum_all(values):
    layers = lax.axis_size("curve") // PLANE
    return pl.pallas_call(
        functools.partial(sum_kernel, layers),
        out_shape=jax.ShapeDtypeStruct(values.shape, jnp.float32),
        in_specs=[pl.BlockSpec(memory_space=pltpu.VMEM)],
        out_specs=pl.BlockSpec(memory_space=pltpu.VMEM),
        scratch_shapes=[
            pltpu.VMEM(values.shape, jnp.float32),
            pltpu.VMEM((PLANE - 1, *values.shape), jnp.float32),
            pltpu.VMEM((layers - 1, *values.shape), jnp.float32),
            pltpu.SemaphoreType.DMA,
            pltpu.SemaphoreType.DMA,
            pltpu.SemaphoreType.DMA,
            pltpu.SemaphoreType.DMA,
        ],
        compiler_params=pltpu.CompilerParams(collective_id=0, has_side_effects=True),
    )(values)


def on_device(atm_flux, ocean_state, area_atm, area_ocean, tiles, tile_row, tile_col, tile_count):
    local_fields, atm_cells = atm_flux.shape
    slot_cap, block_size = (tiles.shape[0], tiles.shape[1])
    atm_span = atm_cells // block_size
    ocean_span = ocean_state.shape[1] // block_size
    margin_blocks = atm_span // 2
    window_span = atm_span + 2 * margin_blocks
    devices = lax.axis_size("curve")
    position = lax.axis_index("curve")
    extended = with_halo(atm_flux, (("curve", 1),), margin_blocks * block_size)
    source_blocks = extended.reshape(local_fields, window_span, block_size)
    weighted_blocks = (ocean_state * area_ocean[None, :]).reshape(
        local_fields, ocean_span, block_size
    )
    local_row = tile_row - position * ocean_span
    local_col = (tile_col - position * atm_span + margin_blocks) % (atm_span * devices)
    live_count = tile_count[0]
    live_slots = (jnp.arange(slot_cap, dtype=jnp.int32) < live_count).astype(jnp.float32)
    ocean_part, window_part = slot_terms(
        tiles,
        local_row,
        local_col,
        live_slots,
        source_blocks,
        weighted_blocks,
        ocean_span,
        window_span,
    )
    ocean_remap = ocean_part.reshape(local_fields, ocean_span * block_size)
    target_ocean = jnp.sum(atm_flux * area_atm[None, :], axis=1)
    got_ocean = jnp.sum(ocean_remap * area_ocean[None, :], axis=1)
    target_atm = jnp.sum(ocean_state * area_ocean[None, :], axis=1)
    window_flat = window_part.reshape(local_fields, window_span * block_size)
    rim_cells = margin_blocks * block_size
    core_cells = atm_span * block_size
    lower_part = window_flat[:, :rim_cells]
    upper_part = window_flat[:, rim_cells + core_cells :]
    core_part = window_flat[:, rim_cells : rim_cells + core_cells]
    from_below = from_behind(upper_part, "curve", 1)
    from_above = from_behind(lower_part, "curve", -1)
    back_sum = core_part + jnp.pad(from_below, ((0, 0), (0, core_cells - rim_cells)))
    back_sum = back_sum + jnp.pad(from_above, ((0, 0), (core_cells - rim_cells, 0)))
    got_atm = jnp.sum(back_sum, axis=1)
    sums = jnp.stack([target_ocean, got_ocean, target_atm, got_atm])
    target_ocean, got_ocean, target_atm, got_atm = sum_all(jnp.pad(sums, ((0, 4), (0, 96))))[:4, :local_fields]
    ocean_flux = ocean_remap * (target_ocean / got_ocean)[:, None]
    atm_fixed = back_sum / area_atm[None, :] * (target_atm / got_atm)[:, None]
    return (ocean_flux, atm_fixed)


def solution(mesh):
    in_specs = (
        P("field", "curve"),
        P("field", "curve"),
        P("curve"),
        P("curve"),
        P("curve", None, None),
        P("curve"),
        P("curve"),
        P("curve"),
    )
    out_specs = (P("field", "curve"), P("field", "curve"))
    return jax.shard_map(
        on_device, mesh=mesh, in_specs=in_specs, out_specs=out_specs, check_vma=False
    )
```

```python
import functools

import jax
import jax.numpy as jnp
from jax import lax
from jax.experimental import pallas as pl
from jax.experimental.pallas import tpu as pltpu
from jax.sharding import PartitionSpec as P

MESH = pl.DeviceIdType.MESH
LANES = 128
CHUNK = 16
GROUP = 8
MIB = 1024 * 1024


def split(values):
    high = values.astype(jnp.bfloat16)
    return high, (values - high.astype(jnp.float32)).astype(jnp.bfloat16)


def twice(block):
    return jnp.concatenate([block, block], axis=1)


def lane_block(index):
    return pl.ds(pl.multiple_of(index * LANES, LANES), LANES)


def remap_kernel(
    flux,
    state,
    area_atm,
    area_ocean,
    tiles,
    tile_row,
    tile_col,
    tile_count,
    ocean_out,
    atm_out,
    sums_out,
    flux_own,
    flux_low,
    flux_high,
    state_own,
    tiles_own,
    tiles_split,
    state_split,
    flux_split,
    back_chain,
    ocean_chain,
    back_core,
    send_low,
    send_high,
    got_low,
    got_high,
    ones_back,
    ocean_own,
    table,
    index,
    mine,
    landed,
    total,
    load_sem,
    tile_sem,
    index_sem,
    store_sem,
    flux_send_sem,
    flux_recv_sem,
    back_send_sem,
    back_recv_sem,
    sum_send_sem,
    sum_recv_sem,
):
    count = lax.axis_size("curve")
    me = lax.axis_index("curve")
    core = lax.axis_index("field")
    above = (lax.rem(me + 1, count), core)
    below = (lax.rem(me + count - 1, count), core)
    fields, atm_cells = flux.shape
    ocean_cells = state.shape[1]
    slots = tiles.shape[0]
    atm_span, ocean_span = atm_cells // LANES, ocean_cells // LANES
    margin = atm_span // 2
    window_span = atm_span + 2 * margin
    rim = margin * LANES

    def partner(step):
        away = (step + 1) // 2
        shift = jnp.where(step % 2 == 0, away, -away)
        return (lax.rem(me + count // 2 + shift + count, count), core)

    barrier = pltpu.get_barrier_semaphore()

    def greet(step, carry):
        pl.semaphore_signal(barrier, inc=1, device_id=partner(step), device_id_type=MESH)
        return carry

    lax.fori_loop(0, count - 1, greet, 0)

    load_state = pltpu.make_async_copy(state, state_own, load_sem.at[0])
    load_flux = pltpu.make_async_copy(flux, flux_own, load_sem.at[1])
    load_state.start()
    load_flux.start()
    chunks = slots // CHUNK

    def load_tiles(chunk):
        part = pl.ds(chunk * CHUNK, CHUNK)
        return pltpu.make_async_copy(tiles.at[part], tiles_own.at[part], tile_sem.at[chunk])

    for chunk in range(chunks):
        load_tiles(chunk).start()

    slot_of_row = lax.broadcasted_iota(jnp.int32, (slots, LANES), 0)
    lane = lax.broadcasted_iota(jnp.int32, (slots, LANES), 1)
    live = slot_of_row < tile_count[0]

    def chain_of(names):
        across = jnp.broadcast_to(names, (slots, LANES))
        down = jnp.transpose(across.astype(jnp.float32)).astype(jnp.int32)
        former = jnp.where((across == down) & (slot_of_row < lane), slot_of_row + 1, 0)
        last = jnp.where((lane == down) & live, slot_of_row + 1, 0)
        return jnp.max(former, axis=0, keepdims=True), jnp.max(last, axis=0, keepdims=True)

    row_names = tile_row[...] - me * ocean_span
    col_names = tile_col[...] - me * atm_span + margin
    ring = atm_span * count
    col_names = jnp.where(col_names < 0, col_names + ring, col_names)
    col_names = jnp.where(col_names >= ring, col_names - ring, col_names)
    row_names = jnp.clip(row_names, 0, ocean_span - 1)
    col_names = jnp.clip(col_names, 0, window_span - 1)
    row_former, row_last = chain_of(row_names)
    col_former, col_last = chain_of(col_names)
    for place, row in enumerate(
        (row_names, col_names, row_former, row_last, col_former, col_last)
    ):
        table[place : place + 1, :] = row
    table[6:8, :] = jnp.zeros((2, LANES), jnp.int32)
    index_copy = pltpu.make_async_copy(table, index, index_sem)
    index_copy.start()

    pl.semaphore_wait(barrier, count - 1)

    def remote(source, target, sends, receives, place, device):
        return pltpu.make_async_remote_copy(
            src_ref=source,
            dst_ref=target,
            send_sem=sends.at[place],
            recv_sem=receives.at[place],
            device_id=device,
            device_id_type=MESH,
        )

    flux_up = remote(
        flux.at[:, pl.ds(atm_cells - rim, rim)], flux_low, flux_send_sem, flux_recv_sem, 0, above
    )
    flux_down = remote(flux.at[:, pl.ds(0, rim)], flux_high, flux_send_sem, flux_recv_sem, 1, below)
    flux_up.start()
    flux_down.start()

    zeros = jnp.zeros((fields, LANES), jnp.float32)
    extra = lax.broadcasted_iota(jnp.int32, (16, LANES), 0)
    load_state.wait()

    def weigh(block, acc):
        area = area_ocean[:, lane_block(block)]
        weighted = state_own[:, lane_block(block)] * area
        high, low = split(weighted)
        state_split[block, 0:fields, :] = high
        state_split[block, fields : 2 * fields, :] = low
        area_high = area.astype(jnp.bfloat16).astype(jnp.float32)
        area_rows = jnp.where(
            extra == 0, area_high, jnp.where(extra == 1, area - area_high, 0.0)
        )
        state_split[block, 2 * fields : 2 * fields + 16, :] = area_rows.astype(jnp.bfloat16)
        return acc + weighted

    target_atm = lax.fori_loop(0, ocean_span, weigh, zeros)

    back_chain[0] = jnp.zeros(back_chain.shape[1:], jnp.float32)
    ocean_chain[0] = jnp.zeros(ocean_chain.shape[1:], jnp.float32)
    index_copy.wait()

    def backward(step, carry):
        for part in range(GROUP):
            slot = step * GROUP + part
            high, low = split(tiles_own[slot])
            tiles_split[slot, 0] = high
            tiles_split[slot, 1] = low
            terms = jnp.dot(
                twice(state_split[index[0, slot]]),
                jnp.concatenate([high, low], axis=0),
                preferred_element_type=jnp.float32,
            )
            former = index[4, slot]
            back_chain[slot + 1, 0:fields, :] = (
                terms[0:fields] + terms[fields : 2 * fields] + back_chain[former, 0:fields, :]
            )
            back_chain[slot + 1, fields : fields + 8, :] = (
                terms[2 * fields : 2 * fields + 8] + back_chain[former, fields : fields + 8, :]
            )
        return carry

    steps = CHUNK // GROUP
    for chunk in range(chunks):
        load_tiles(chunk).wait()
        lax.fori_loop(chunk * steps, (chunk + 1) * steps, backward, 0)

    def collect(target, first):
        def one(block, acc):
            slot = index[5, first + block]
            sums = back_chain[slot, 0:fields, :]
            target[:, lane_block(block)] = sums
            ones_back[first + block] = jnp.sum(
                back_chain[slot, fields : fields + 8, :], axis=0, keepdims=True
            )
            return acc + sums

        return one

    got_atm = lax.fori_loop(0, margin, collect(send_low, 0), zeros)
    back_down = remote(send_low, got_high, back_send_sem, back_recv_sem, 1, below)
    back_down.start()
    got_atm = lax.fori_loop(0, margin, collect(send_high, margin + atm_span), got_atm)
    back_up = remote(send_high, got_low, back_send_sem, back_recv_sem, 0, above)
    back_up.start()
    got_atm = lax.fori_loop(0, atm_span, collect(back_core, margin), got_atm)

    load_flux.wait()

    def spread(source, first, own):
        def one(block, acc):
            values = source[:, lane_block(block)]
            high, low = split(values)
            flux_split[first + block, 0:fields, :] = high
            flux_split[first + block, fields : 2 * fields, :] = low
            got = acc[1] + values * ones_back[first + block]
            if own:
                return acc[0] + values * area_atm[:, lane_block(block)], got
            return acc[0], got

        return one

    acc = lax.fori_loop(0, atm_span, spread(flux_own, margin, True), (zeros, zeros))
    flux_up.wait_recv()
    flux_down.wait_recv()
    acc = lax.fori_loop(0, margin, spread(flux_low, 0, False), acc)
    target_ocean, got_ocean = lax.fori_loop(
        0, margin, spread(flux_high, margin + atm_span, False), acc
    )

    stacked = jnp.concatenate([target_ocean, got_ocean, target_atm, got_atm], axis=0)
    mine[...] = jnp.sum(jnp.transpose(stacked), axis=0, keepdims=True)

    def send_row(step, carry):
        pltpu.make_async_remote_copy(
            src_ref=mine,
            dst_ref=landed.at[step],
            send_sem=sum_send_sem,
            recv_sem=sum_recv_sem,
            device_id=partner(step),
            device_id_type=MESH,
        ).start()
        return carry

    lax.fori_loop(0, count - 1, send_row, 0)

    def forward(step, carry):
        for part in range(GROUP):
            slot = step * GROUP + part
            terms = lax.dot_general(
                twice(flux_split[index[1, slot]]),
                jnp.concatenate([tiles_split[slot, 0], tiles_split[slot, 1]], axis=1),
                (((1,), (1,)), ((), ())),
                preferred_element_type=jnp.float32,
            )
            ocean_chain[slot + 1] = (
                terms[0:fields] + terms[fields : 2 * fields] + ocean_chain[index[2, slot]]
            )
        return carry

    lax.fori_loop(0, slots // GROUP, forward, 0)

    def place_ocean(block, carry):
        ocean_own[:, lane_block(block)] = ocean_chain[index[3, block]]
        return carry

    lax.fori_loop(0, ocean_span, place_ocean, 0)
    store_ocean = pltpu.make_async_copy(ocean_own, ocean_out, store_sem.at[0])
    store_ocean.start()

    back_up.wait_recv()
    back_down.wait_recv()
    half = atm_cells - rim
    back_core[:, 0:rim] = (back_core[:, 0:rim] + got_low[...]) / area_atm[:, 0:rim]
    back_core[:, half:] = (back_core[:, half:] + got_high[...]) / area_atm[:, half:]
    store_atm = pltpu.make_async_copy(back_core, atm_out, store_sem.at[1])
    store_atm.start()

    pltpu.make_async_copy(landed, landed, sum_recv_sem).wait()
    total[...] = mine[...] + jnp.sum(landed[...], axis=0)
    store_sums = pltpu.make_async_copy(total, sums_out, store_sem.at[2])
    store_sums.start()
    for copy in (flux_up, flux_down, back_up, back_down):
        copy.wait_send()
    pltpu.make_async_copy(landed, landed, sum_send_sem).wait()
    store_ocean.wait()
    store_atm.wait()
    store_sums.wait()


def scale_kernel(ocean, atm, sums, ocean_out, atm_out):
    fields = ocean.shape[0]
    columns = jnp.transpose(jnp.broadcast_to(sums[...], (LANES, LANES)))
    target_ocean, got_ocean, target_atm, got_atm = (
        columns[part * fields : (part + 1) * fields, 0:1] for part in range(4)
    )
    ocean_out[...] = ocean[...] * (target_ocean / got_ocean)
    atm_out[...] = atm[...] * (target_atm / got_atm)


def on_device(atm_flux, ocean_state, area_atm, area_ocean, tiles, tile_row, tile_col, tile_count):
    fields, atm_cells = atm_flux.shape
    ocean_cells = ocean_state.shape[1]
    slots = tiles.shape[0]
    devices = lax.axis_size("curve")
    atm_span, ocean_span = atm_cells // LANES, ocean_cells // LANES
    margin = atm_span // 2
    window_span = atm_span + 2 * margin
    rim = margin * LANES
    f32, bf16 = jnp.float32, jnp.bfloat16
    anywhere = pl.BlockSpec(memory_space=pl.ANY)
    vmem = pl.BlockSpec(memory_space=pltpu.VMEM)
    smem = pl.BlockSpec(memory_space=pltpu.SMEM)
    ocean_raw, atm_raw, sums = pl.pallas_call(
        remap_kernel,
        out_shape=(
            jax.ShapeDtypeStruct((fields, ocean_cells), f32),
            jax.ShapeDtypeStruct((fields, atm_cells), f32),
            jax.ShapeDtypeStruct((1, LANES), f32),
        ),
        in_specs=[anywhere, anywhere, vmem, vmem, anywhere, vmem, vmem, smem],
        out_specs=(anywhere, anywhere, anywhere),
        scratch_shapes=[
            pltpu.VMEM((fields, atm_cells), f32),
            pltpu.VMEM((fields, rim), f32),
            pltpu.VMEM((fields, rim), f32),
            pltpu.VMEM((fields, ocean_cells), f32),
            pltpu.VMEM(tiles.shape, f32),
            pltpu.VMEM((slots, 2, LANES, LANES), bf16),
            pltpu.VMEM((ocean_span, 2 * fields + 16, LANES), bf16),
            pltpu.VMEM((window_span, 2 * fields, LANES), bf16),
            pltpu.VMEM((slots + 1, fields + 8, LANES), f32),
            pltpu.VMEM((slots + 1, fields, LANES), f32),
            pltpu.VMEM((fields, atm_cells), f32),
            pltpu.VMEM((fields, rim), f32),
            pltpu.VMEM((fields, rim), f32),
            pltpu.VMEM((fields, rim), f32),
            pltpu.VMEM((fields, rim), f32),
            pltpu.VMEM((window_span, 1, LANES), f32),
            pltpu.VMEM((fields, ocean_cells), f32),
            pltpu.VMEM((8, LANES), jnp.int32),
            pltpu.SMEM((8, LANES), jnp.int32),
            pltpu.VMEM((1, LANES), f32),
            pltpu.VMEM((devices - 1, 1, LANES), f32),
            pltpu.VMEM((1, LANES), f32),
            pltpu.SemaphoreType.DMA((2,)),
            pltpu.SemaphoreType.DMA((slots // CHUNK,)),
            pltpu.SemaphoreType.DMA,
            pltpu.SemaphoreType.DMA((3,)),
            pltpu.SemaphoreType.DMA((2,)),
            pltpu.SemaphoreType.DMA((2,)),
            pltpu.SemaphoreType.DMA((2,)),
            pltpu.SemaphoreType.DMA((2,)),
            pltpu.SemaphoreType.DMA,
            pltpu.SemaphoreType.DMA,
        ],
        compiler_params=pltpu.CompilerParams(
            collective_id=0, has_side_effects=True, vmem_limit_bytes=48 * MIB
        ),
        name="remap",
    )(
        atm_flux,
        ocean_state,
        area_atm.reshape(1, atm_cells),
        area_ocean.reshape(1, ocean_cells),
        tiles,
        tile_row.reshape(1, slots),
        tile_col.reshape(1, slots),
        tile_count,
    )
    return pl.pallas_call(
        scale_kernel,
        grid=(4,),
        out_shape=(
            jax.ShapeDtypeStruct((fields, ocean_cells), f32),
            jax.ShapeDtypeStruct((fields, atm_cells), f32),
        ),
        in_specs=[
            pl.BlockSpec((fields, ocean_cells // 4), lambda step: (0, step)),
            pl.BlockSpec((fields, atm_cells // 4), lambda step: (0, step)),
            pl.BlockSpec((1, LANES), lambda step: (0, 0)),
        ],
        out_specs=(
            pl.BlockSpec((fields, ocean_cells // 4), lambda step: (0, step)),
            pl.BlockSpec((fields, atm_cells // 4), lambda step: (0, step)),
        ),
        name="scale",
    )(ocean_raw, atm_raw, sums)


def solution(mesh):
    in_specs = (
        P("field", "curve"),
        P("field", "curve"),
        P("curve"),
        P("curve"),
        P("curve", None, None),
        P("curve"),
        P("curve"),
        P("curve"),
    )
    out_specs = (P("field", "curve"), P("field", "curve"))
    return jax.shard_map(
        on_device, mesh=mesh, in_specs=in_specs, out_specs=out_specs, check_vma=False
    )
```

```python
import functools

import jax
import jax.numpy as jnp
from jax import lax
from jax.experimental import pallas as pl
from jax.experimental.pallas import tpu as pltpu
from jax.sharding import PartitionSpec as P

MESH = pl.DeviceIdType.MESH
LANES = 128
PLANE = 16
CHUNK = 16
GROUP = 8
MIB = 1024 * 1024


def split(values):
    high = values.astype(jnp.bfloat16)
    return high, (values - high.astype(jnp.float32)).astype(jnp.bfloat16)


def twice(block):
    return jnp.concatenate([block, block], axis=1)


def lane_block(index):
    return pl.ds(pl.multiple_of(index * LANES, LANES), LANES)


def remap_kernel(
    flux,
    state,
    area_atm_in,
    area_ocean_in,
    tiles,
    tile_row_in,
    tile_col_in,
    tile_count,
    ocean_own,
    back_core,
    ratios,
    area_atm,
    area_ocean,
    tile_row,
    tile_col,
    flux_own,
    flux_low,
    flux_high,
    state_own,
    tiles_own,
    tiles_split,
    state_split,
    flux_split,
    back_chain,
    ocean_chain,
    send_low,
    send_high,
    got_low,
    got_high,
    ones_back,
    ones_low,
    ones_high,
    table,
    index,
    mine,
    landed,
    entered,
    load_sem,
    tile_sem,
    index_sem,
    flux_send_sem,
    flux_recv_sem,
    ones_send_sem,
    ones_recv_sem,
    back_send_sem,
    back_recv_sem,
    sum_send_sem,
    sum_recv_sem,
):
    count = lax.axis_size("curve")
    me = lax.axis_index("curve")
    core = lax.axis_index("field")
    above = (lax.rem(me + 1, count), core)
    below = (lax.rem(me + count - 1, count), core)
    fields, atm_cells = flux.shape
    ocean_cells = state.shape[1]
    slots = tiles.shape[0]
    atm_span, ocean_span = atm_cells // LANES, ocean_cells // LANES
    margin = atm_span // 2
    window_span = atm_span + 2 * margin
    rim = margin * LANES

    layers = count // PLANE
    layer, place = me // PLANE, me % PLANE

    def partner(step):
        away = (step + 1) // 2
        shift = jnp.where(step % 2 == 0, away, -away)
        return (lax.rem(me + count // 2 + shift + count, count), core)

    def plane_partner(step):
        return (layer * PLANE + lax.rem(place + step, PLANE), core)

    def line_partner(step):
        return (lax.rem(layer + step, layers) * PLANE + place, core)

    barrier = pltpu.get_barrier_semaphore()

    def greet(semaphore, partner_of):
        def one(step, carry):
            pl.semaphore_signal(semaphore, inc=1, device_id=partner_of(step), device_id_type=MESH)
            return carry

        return one

    for neighbour in (above, below):
        pl.semaphore_signal(barrier, inc=1, device_id=neighbour, device_id_type=MESH)
    lax.fori_loop(1, layers, greet(barrier, line_partner), 0)
    lax.fori_loop(1, PLANE, greet(barrier, plane_partner), 0)

    loads = [
        pltpu.make_async_copy(source, target, load_sem.at[place])
        for place, (source, target) in enumerate(
            (
                (tile_row_in, tile_row),
                (tile_col_in, tile_col),
                (area_ocean_in, area_ocean),
                (state, state_own),
                (area_atm_in, area_atm),
                (flux, flux_own),
            )
        )
    ]
    for load in loads:
        load.start()
    chunks = slots // CHUNK

    def load_tiles(chunk):
        part = pl.ds(chunk * CHUNK, CHUNK)
        return pltpu.make_async_copy(tiles.at[part], tiles_own.at[part], tile_sem.at[chunk])

    for chunk in range(chunks):
        load_tiles(chunk).start()

    for load in loads[0:2]:
        load.wait()
    slot_of_row = lax.broadcasted_iota(jnp.int32, (slots, LANES), 0)
    lane = lax.broadcasted_iota(jnp.int32, (slots, LANES), 1)
    live = slot_of_row < tile_count[0]

    def chain_of(names):
        across = jnp.broadcast_to(names, (slots, LANES))
        down = jnp.transpose(across.astype(jnp.float32)).astype(jnp.int32)
        former = jnp.where((across == down) & (slot_of_row < lane), slot_of_row + 1, 0)
        last = jnp.where((lane == down) & live, slot_of_row + 1, 0)
        return jnp.max(former, axis=0, keepdims=True), jnp.max(last, axis=0, keepdims=True)

    row_names = tile_row[...] - me * ocean_span
    col_names = tile_col[...] - me * atm_span + margin
    ring = atm_span * count
    col_names = jnp.where(col_names < 0, col_names + ring, col_names)
    col_names = jnp.where(col_names >= ring, col_names - ring, col_names)
    row_names = jnp.clip(row_names, 0, ocean_span - 1)
    col_names = jnp.clip(col_names, 0, window_span - 1)
    row_former, row_last = chain_of(row_names)
    col_former, col_last = chain_of(col_names)
    for line, row in enumerate(
        (row_names, col_names, row_former, row_last, col_former, col_last)
    ):
        table[line : line + 1, :] = row
    table[6:8, :] = jnp.zeros((2, LANES), jnp.int32)
    index_copy = pltpu.make_async_copy(table, index, index_sem)
    index_copy.start()

    pl.semaphore_wait(barrier, PLANE + layers)
    lax.fori_loop(1, layers, greet(entered, line_partner), 0)

    def remote(source, target, sends, receives, place, device):
        return pltpu.make_async_remote_copy(
            src_ref=source,
            dst_ref=target,
            send_sem=sends.at[place],
            recv_sem=receives.at[place],
            device_id=device,
            device_id_type=MESH,
        )

    flux_up = remote(
        flux.at[:, pl.ds(atm_cells - rim, rim)], flux_low, flux_send_sem, flux_recv_sem, 0, above
    )
    flux_down = remote(flux.at[:, pl.ds(0, rim)], flux_high, flux_send_sem, flux_recv_sem, 1, below)
    flux_up.start()
    flux_down.start()

    zeros = jnp.zeros((fields, LANES), jnp.float32)
    extra = lax.broadcasted_iota(jnp.int32, (16, LANES), 0)
    for load in loads[2:4]:
        load.wait()

    def weigh(block, acc):
        area = area_ocean[:, lane_block(block)]
        weighted = state_own[:, lane_block(block)] * area
        high, low = split(weighted)
        state_split[block, 0:fields, :] = high
        state_split[block, fields : 2 * fields, :] = low
        area_high = area.astype(jnp.bfloat16).astype(jnp.float32)
        area_rows = jnp.where(
            extra == 0, area_high, jnp.where(extra == 1, area - area_high, 0.0)
        )
        state_split[block, 2 * fields : 2 * fields + 16, :] = area_rows.astype(jnp.bfloat16)
        return acc + weighted

    target_atm = lax.fori_loop(0, ocean_span, weigh, zeros)

    back_chain[0] = jnp.zeros(back_chain.shape[1:], jnp.float32)
    ocean_chain[0] = jnp.zeros(ocean_chain.shape[1:], jnp.float32)
    index_copy.wait()

    def backward(step, carry):
        for part in range(GROUP):
            slot = step * GROUP + part
            high, low = split(tiles_own[slot])
            tiles_split[slot, 0] = high
            tiles_split[slot, 1] = low
            terms = jnp.dot(
                twice(state_split[index[0, slot]]),
                jnp.concatenate([high, low], axis=0),
                preferred_element_type=jnp.float32,
            )
            former = index[4, slot]
            back_chain[slot + 1, 0:fields, :] = (
                terms[0:fields] + terms[fields : 2 * fields] + back_chain[former, 0:fields, :]
            )
            back_chain[slot + 1, fields : fields + 8, :] = (
                terms[2 * fields : 2 * fields + 8] + back_chain[former, fields : fields + 8, :]
            )
        return carry

    steps = CHUNK // GROUP
    for chunk in range(chunks):
        load_tiles(chunk).wait()
        lax.fori_loop(chunk * steps, (chunk + 1) * steps, backward, 0)

    def collect(target, first):
        def one(block, acc):
            slot = index[5, first + block]
            sums = back_chain[slot, 0:fields, :]
            target[:, lane_block(block)] = sums
            ones_back[first + block] = jnp.sum(
                back_chain[slot, fields : fields + 8, :], axis=0, keepdims=True
            )
            return acc + sums

        return one

    got_atm = lax.fori_loop(0, margin, collect(send_low, 0), zeros)
    got_atm = lax.fori_loop(0, margin, collect(send_high, margin + atm_span), got_atm)
    ones_down = remote(
        ones_back.at[pl.ds(0, margin)], ones_high, ones_send_sem, ones_recv_sem, 1, below
    )
    ones_up = remote(
        ones_back.at[pl.ds(margin + atm_span, margin)],
        ones_low,
        ones_send_sem,
        ones_recv_sem,
        0,
        above,
    )
    ones_down.start()
    ones_up.start()
    back_down = remote(send_low, got_high, back_send_sem, back_recv_sem, 1, below)
    back_up = remote(send_high, got_low, back_send_sem, back_recv_sem, 0, above)
    back_down.start()
    back_up.start()
    got_atm = lax.fori_loop(0, atm_span, collect(back_core, margin), got_atm)

    for load in loads[4:6]:
        load.wait()

    def spread(source, first):
        def one(block, carry):
            high, low = split(source[:, lane_block(block)])
            flux_split[first + block, 0:fields, :] = high
            flux_split[first + block, fields : 2 * fields, :] = low
            return carry

        return one

    def integrate(first, factors):
        def one(block, acc):
            return acc + flux_own[:, lane_block(first + block)] * factors(block)

        return one

    lax.fori_loop(0, atm_span, spread(flux_own, margin), 0)
    target_ocean = lax.fori_loop(
        0, atm_span, integrate(0, lambda block: area_atm[:, lane_block(block)]), zeros
    )
    ones_up.wait_recv()
    ones_down.wait_recv()
    got_ocean = lax.fori_loop(
        0, margin, integrate(0, lambda block: ones_back[margin + block] + ones_low[block]), zeros
    )
    got_ocean = lax.fori_loop(
        0,
        margin,
        integrate(margin, lambda block: ones_back[2 * margin + block] + ones_high[block]),
        got_ocean,
    )

    stacked = jnp.concatenate([target_ocean, got_ocean, target_atm, got_atm], axis=0)
    mine[...] = jnp.sum(jnp.transpose(stacked), axis=0, keepdims=True)

    def send_row(step, carry):
        pltpu.make_async_remote_copy(
            src_ref=mine,
            dst_ref=landed.at[step],
            send_sem=sum_send_sem,
            recv_sem=sum_recv_sem,
            device_id=partner(step),
            device_id_type=MESH,
        ).start()
        return carry

    pl.semaphore_wait(entered, layers - 1)
    lax.fori_loop(0, count - 1, send_row, 0)

    flux_up.wait_recv()
    flux_down.wait_recv()
    lax.fori_loop(0, margin, spread(flux_low, 0), 0)
    lax.fori_loop(0, margin, spread(flux_high, margin + atm_span), 0)

    def forward(step, carry):
        for part in range(GROUP):
            slot = step * GROUP + part
            terms = lax.dot_general(
                twice(flux_split[index[1, slot]]),
                jnp.concatenate([tiles_split[slot, 0], tiles_split[slot, 1]], axis=1),
                (((1,), (1,)), ((), ())),
                preferred_element_type=jnp.float32,
            )
            ocean_chain[slot + 1] = (
                terms[0:fields] + terms[fields : 2 * fields] + ocean_chain[index[2, slot]]
            )
        return carry

    lax.fori_loop(0, slots // GROUP, forward, 0)

    def place_ocean(block, carry):
        ocean_own[:, lane_block(block)] = ocean_chain[index[3, block]]
        return carry

    lax.fori_loop(0, ocean_span, place_ocean, 0)

    back_up.wait_recv()
    back_down.wait_recv()
    half = atm_cells - rim
    back_core[:, 0:rim] = (back_core[:, 0:rim] + got_low[...]) / area_atm[:, 0:rim]
    back_core[:, half:] = (back_core[:, half:] + got_high[...]) / area_atm[:, half:]

    pltpu.make_async_copy(landed, landed, sum_recv_sem).wait()
    sums = mine[...] + jnp.sum(landed[...], axis=0)
    columns = jnp.transpose(jnp.broadcast_to(sums, (LANES, LANES)))
    ratios[0] = columns[0:fields] / columns[fields : 2 * fields]
    ratios[1] = columns[2 * fields : 3 * fields] / columns[3 * fields :]
    for copy in (flux_up, flux_down, ones_up, ones_down, back_up, back_down):
        copy.wait_send()
    pltpu.make_async_copy(landed, landed, sum_send_sem).wait()


def scale_kernel(ocean, atm, ratios, ocean_out, atm_out, ocean_own, atm_own, store_sem):
    stores = []
    for part in range(ocean.shape[0] // 8):
        rows = pl.ds(part * 8, 8)
        for place, (source, own, target) in enumerate(
            ((ocean, ocean_own, ocean_out), (atm, atm_own, atm_out))
        ):
            ratio = ratios[place, rows, :]
            for block in range(source.shape[1] // LANES):
                cells = pl.ds(block * LANES, LANES)
                own[rows, cells] = source[rows, cells] * ratio
            stores.append(
                pltpu.make_async_copy(own.at[rows], target.at[rows], store_sem.at[part, place])
            )
            stores[-1].start()
    for store in stores:
        store.wait()


def on_device(atm_flux, ocean_state, area_atm, area_ocean, tiles, tile_row, tile_col, tile_count):
    fields, atm_cells = atm_flux.shape
    ocean_cells = ocean_state.shape[1]
    slots = tiles.shape[0]
    devices = lax.axis_size("curve")
    atm_span, ocean_span = atm_cells // LANES, ocean_cells // LANES
    margin = atm_span // 2
    window_span = atm_span + 2 * margin
    rim = margin * LANES
    f32, bf16 = jnp.float32, jnp.bfloat16
    hbm = pl.BlockSpec(memory_space=pltpu.HBM)
    vmem = pl.BlockSpec(memory_space=pltpu.VMEM)
    ocean_raw, atm_raw, ratios = pl.pallas_call(
        remap_kernel,
        out_shape=(
            pltpu.VMEM((fields, ocean_cells), f32),
            pltpu.VMEM((fields, atm_cells), f32),
            pltpu.VMEM((2, fields, LANES), f32),
        ),
        in_specs=[hbm] * 7 + [pl.BlockSpec(memory_space=pltpu.SMEM)],
        out_specs=(vmem, vmem, vmem),
        scratch_shapes=[
            pltpu.VMEM((1, atm_cells), f32),
            pltpu.VMEM((1, ocean_cells), f32),
            pltpu.VMEM((1, slots), jnp.int32),
            pltpu.VMEM((1, slots), jnp.int32),
            pltpu.VMEM((fields, atm_cells), f32),
            pltpu.VMEM((fields, rim), f32),
            pltpu.VMEM((fields, rim), f32),
            pltpu.VMEM((fields, ocean_cells), f32),
            pltpu.VMEM(tiles.shape, f32),
            pltpu.VMEM((slots, 2, LANES, LANES), bf16),
            pltpu.VMEM((ocean_span, 2 * fields + 16, LANES), bf16),
            pltpu.VMEM((window_span, 2 * fields, LANES), bf16),
            pltpu.VMEM((slots + 1, fields + 8, LANES), f32),
            pltpu.VMEM((slots + 1, fields, LANES), f32),
            pltpu.VMEM((fields, rim), f32),
            pltpu.VMEM((fields, rim), f32),
            pltpu.VMEM((fields, rim), f32),
            pltpu.VMEM((fields, rim), f32),
            pltpu.VMEM((window_span, 1, LANES), f32),
            pltpu.VMEM((margin, 1, LANES), f32),
            pltpu.VMEM((margin, 1, LANES), f32),
            pltpu.VMEM((8, LANES), jnp.int32),
            pltpu.SMEM((8, LANES), jnp.int32),
            pltpu.VMEM((1, LANES), f32),
            pltpu.VMEM((devices - 1, 1, LANES), f32),
            pltpu.SemaphoreType.REGULAR,
            pltpu.SemaphoreType.DMA((6,)),
            pltpu.SemaphoreType.DMA((slots // CHUNK,)),
            pltpu.SemaphoreType.DMA,
            pltpu.SemaphoreType.DMA((2,)),
            pltpu.SemaphoreType.DMA((2,)),
            pltpu.SemaphoreType.DMA((2,)),
            pltpu.SemaphoreType.DMA((2,)),
            pltpu.SemaphoreType.DMA((2,)),
            pltpu.SemaphoreType.DMA((2,)),
            pltpu.SemaphoreType.DMA,
            pltpu.SemaphoreType.DMA,
        ],
        compiler_params=pltpu.CompilerParams(
            collective_id=0, has_side_effects=True, vmem_limit_bytes=40 * MIB
        ),
        name="remap",
    )(
        *(
            pltpu.with_memory_space_constraint(operand, pltpu.HBM)
            for operand in (
                atm_flux,
                ocean_state,
                area_atm.reshape(1, atm_cells),
                area_ocean.reshape(1, ocean_cells),
                tiles,
                tile_row.reshape(1, slots),
                tile_col.reshape(1, slots),
            )
        ),
        tile_count,
    )
    return pl.pallas_call(
        scale_kernel,
        out_shape=(
            jax.ShapeDtypeStruct((fields, ocean_cells), f32),
            jax.ShapeDtypeStruct((fields, atm_cells), f32),
        ),
        in_specs=[vmem] * 3,
        out_specs=(hbm, hbm),
        scratch_shapes=[
            pltpu.VMEM((fields, ocean_cells), f32),
            pltpu.VMEM((fields, atm_cells), f32),
            pltpu.SemaphoreType.DMA((fields // 8, 2)),
        ],
        compiler_params=pltpu.CompilerParams(vmem_limit_bytes=8 * MIB),
        name="scale",
    )(ocean_raw, atm_raw, ratios)


def solution(mesh):
    in_specs = (
        P("field", "curve"),
        P("field", "curve"),
        P("curve"),
        P("curve"),
        P("curve", None, None),
        P("curve"),
        P("curve"),
        P("curve"),
    )
    out_specs = (P("field", "curve"), P("field", "curve"))
    return jax.shard_map(
        on_device, mesh=mesh, in_specs=in_specs, out_specs=out_specs, check_vma=False
    )
```

```python
import functools

import jax
import jax.numpy as jnp
from jax import lax
from jax.experimental import pallas as pl
from jax.experimental.pallas import tpu as pltpu
from jax.sharding import PartitionSpec as P

MESH = pl.DeviceIdType.MESH
LANES = 128
PLANE = 16
CHUNK = 32
MIB = 1024 * 1024


def split(values):
    high = values.astype(jnp.bfloat16)
    return high, (values - high.astype(jnp.float32)).astype(jnp.bfloat16)


def twice(block):
    return jnp.concatenate([block, block], axis=1)


def lane_block(index):
    return pl.ds(pl.multiple_of(index * LANES, LANES), LANES)


def remap_kernel(
    flux,
    state,
    area_atm_in,
    area_ocean_in,
    tiles,
    tile_row_in,
    tile_col_in,
    tile_count,
    ocean_own,
    back_core,
    ratios,
    area_atm,
    area_ocean,
    tile_row,
    tile_col,
    flux_own,
    flux_low,
    flux_high,
    state_own,
    tiles_own,
    tiles_turned,
    state_split,
    flux_split,
    back_chain,
    ocean_chain,
    send_low,
    send_high,
    got_low,
    got_high,
    ones_back,
    ones_low,
    ones_high,
    table,
    index,
    mine,
    landed,
    entered,
    load_sem,
    tile_sem,
    index_sem,
    flux_send_sem,
    flux_recv_sem,
    ones_send_sem,
    ones_recv_sem,
    back_send_sem,
    back_recv_sem,
    sum_send_sem,
    sum_recv_sem,
):
    count = lax.axis_size("curve")
    me = lax.axis_index("curve")
    core = lax.axis_index("field")
    above = (lax.rem(me + 1, count), core)
    below = (lax.rem(me + count - 1, count), core)
    fields, atm_cells = flux.shape
    ocean_cells = state.shape[1]
    slots = tiles.shape[0]
    atm_span, ocean_span = atm_cells // LANES, ocean_cells // LANES
    margin = atm_span // 2
    window_span = atm_span + 2 * margin
    rim = margin * LANES

    layers = count // PLANE
    layer, place = me // PLANE, me % PLANE

    def partner(step):
        away = (step + 1) // 2
        shift = jnp.where(step % 2 == 0, away, -away)
        return (lax.rem(me + count // 2 + shift + count, count), core)

    def plane_partner(step):
        return (layer * PLANE + lax.rem(place + step, PLANE), core)

    def line_partner(step):
        return (lax.rem(layer + step, layers) * PLANE + place, core)

    barrier = pltpu.get_barrier_semaphore()

    def greet(semaphore, partner_of):
        def one(step, carry):
            pl.semaphore_signal(semaphore, inc=1, device_id=partner_of(step), device_id_type=MESH)
            return carry

        return one

    for neighbour in (above, below):
        pl.semaphore_signal(barrier, inc=1, device_id=neighbour, device_id_type=MESH)
    lax.fori_loop(1, layers, greet(barrier, line_partner), 0)
    lax.fori_loop(1, PLANE, greet(barrier, plane_partner), 0)

    loads = [
        pltpu.make_async_copy(source, target, load_sem.at[place])
        for place, (source, target) in enumerate(
            (
                (tile_row_in, tile_row),
                (tile_col_in, tile_col),
                (area_ocean_in, area_ocean),
                (state, state_own),
                (area_atm_in, area_atm),
                (flux, flux_own),
            )
        )
    ]
    for load in loads[0:4]:
        load.start()
    chunks = slots // CHUNK

    def load_tiles(chunk):
        part = pl.ds(chunk * CHUNK, CHUNK)
        return pltpu.make_async_copy(tiles.at[part], tiles_own.at[part], tile_sem.at[chunk])

    for chunk in range(chunks):
        load_tiles(chunk).start()
    for load in loads[4:6]:
        load.start()

    for load in loads[0:2]:
        load.wait()
    slot_of_row = lax.broadcasted_iota(jnp.int32, (slots, LANES), 0)
    lane = lax.broadcasted_iota(jnp.int32, (slots, LANES), 1)
    live = slot_of_row < tile_count[0]

    def chain_of(names):
        across = jnp.broadcast_to(names, (slots, LANES))
        down = jnp.transpose(across.astype(jnp.float32)).astype(jnp.int32)
        former = jnp.where((across == down) & (slot_of_row < lane), slot_of_row + 1, 0)
        last = jnp.where((lane == down) & live, slot_of_row + 1, 0)
        return jnp.max(former, axis=0, keepdims=True), jnp.max(last, axis=0, keepdims=True)

    row_names = tile_row[...] - me * ocean_span
    col_names = tile_col[...] - me * atm_span + margin
    ring = atm_span * count
    col_names = jnp.where(col_names < 0, col_names + ring, col_names)
    col_names = jnp.where(col_names >= ring, col_names - ring, col_names)
    row_names = jnp.clip(row_names, 0, ocean_span - 1)
    col_names = jnp.clip(col_names, 0, window_span - 1)
    row_former, row_last = chain_of(row_names)
    col_former, col_last = chain_of(col_names)
    for line, row in enumerate(
        (row_names, col_names, row_former, row_last, col_former, col_last)
    ):
        table[line : line + 1, :] = row
    table[6:8, :] = jnp.zeros((2, LANES), jnp.int32)
    index_copy = pltpu.make_async_copy(table, index, index_sem)
    index_copy.start()

    def remote(source, target, sends, receives, place, device):
        return pltpu.make_async_remote_copy(
            src_ref=source,
            dst_ref=target,
            send_sem=sends.at[place],
            recv_sem=receives.at[place],
            device_id=device,
            device_id_type=MESH,
        )

    pl.semaphore_wait(barrier, PLANE + layers)
    lax.fori_loop(1, layers, greet(entered, line_partner), 0)

    half_fields = fields // 2
    flux_sends = []
    for half in range(2):
        rows = pl.ds(half * half_fields, half_fields)
        flux_sends.append(
            (
                remote(
                    flux.at[rows, pl.ds(atm_cells - rim, rim)],
                    flux_low.at[rows],
                    flux_send_sem,
                    flux_recv_sem,
                    2 * half,
                    above,
                ),
                remote(
                    flux.at[rows, pl.ds(0, rim)],
                    flux_high.at[rows],
                    flux_send_sem,
                    flux_recv_sem,
                    2 * half + 1,
                    below,
                ),
            )
        )
    for copy in flux_sends[0]:
        copy.start()

    zeros = jnp.zeros((fields, LANES), jnp.float32)
    extra = lax.broadcasted_iota(jnp.int32, (16, LANES), 0)
    for load in loads[2:4]:
        load.wait()

    def weigh(block, acc):
        area = area_ocean[:, lane_block(block)]
        weighted = state_own[:, lane_block(block)] * area
        high, low = split(weighted)
        state_split[block, 0:fields, :] = high
        state_split[block, fields : 2 * fields, :] = low
        area_high = area.astype(jnp.bfloat16).astype(jnp.float32)
        area_rows = jnp.where(
            extra == 0, area_high, jnp.where(extra == 1, area - area_high, 0.0)
        )
        state_split[block, 2 * fields : 2 * fields + 16, :] = area_rows.astype(jnp.bfloat16)
        return acc + weighted

    target_atm = lax.fori_loop(0, ocean_span, weigh, zeros, unroll=8)

    back_chain[0] = jnp.zeros(back_chain.shape[1:], jnp.float32)
    ocean_chain[0] = jnp.zeros(ocean_chain.shape[1:], jnp.float32)
    index_copy.wait()

    def backward(chunk, carry):
        load_tiles(chunk).wait()
        for part in range(CHUNK):
            slot = chunk * CHUNK + part
            weights = tiles_own[slot]
            high, low = split(weights.T)
            tiles_turned[slot, 0] = high
            tiles_turned[slot, 1] = low
            terms = jnp.dot(
                twice(state_split[index[0, slot]]),
                jnp.concatenate(split(weights), axis=0),
                preferred_element_type=jnp.float32,
            )
            former = index[4, slot]
            back_chain[slot + 1, 0:fields, :] = (
                terms[0:fields] + terms[fields : 2 * fields] + back_chain[former, 0:fields, :]
            )
            back_chain[slot + 1, fields : fields + 8, :] = (
                terms[2 * fields : 2 * fields + 8] + back_chain[former, fields : fields + 8, :]
            )
        return carry

    lax.fori_loop(0, chunks, backward, 0)

    def collect(target, first):
        def one(block, acc):
            slot = index[5, first + block]
            sums = back_chain[slot, 0:fields, :]
            target[:, lane_block(block)] = sums
            ones_back[first + block] = jnp.sum(
                back_chain[slot, fields : fields + 8, :], axis=0, keepdims=True
            )
            return acc + sums

        return one

    got_atm = lax.fori_loop(0, margin, collect(send_low, 0), zeros, unroll=8)
    got_atm = lax.fori_loop(0, margin, collect(send_high, margin + atm_span), got_atm, unroll=8)
    ones_down = remote(
        ones_back.at[pl.ds(0, margin)], ones_high, ones_send_sem, ones_recv_sem, 1, below
    )
    ones_up = remote(
        ones_back.at[pl.ds(margin + atm_span, margin)],
        ones_low,
        ones_send_sem,
        ones_recv_sem,
        0,
        above,
    )
    ones_down.start()
    ones_up.start()
    for copy in flux_sends[1]:
        copy.start()
    back_down = remote(send_low, got_high, back_send_sem, back_recv_sem, 1, below)
    back_up = remote(send_high, got_low, back_send_sem, back_recv_sem, 0, above)
    back_down.start()
    back_up.start()
    got_atm = lax.fori_loop(0, atm_span, collect(back_core, margin), got_atm, unroll=8)

    for load in loads[4:6]:
        load.wait()

    def spread(source, first):
        def one(block, carry):
            high, low = split(source[:, lane_block(block)])
            flux_split[first + block, 0:fields, :] = high
            flux_split[first + block, fields : 2 * fields, :] = low
            return carry

        return one

    def integrate(first, factors):
        def one(block, acc):
            return acc + flux_own[:, lane_block(first + block)] * factors(block)

        return one

    lax.fori_loop(0, atm_span, spread(flux_own, margin), 0, unroll=8)
    target_ocean = lax.fori_loop(
        0, atm_span, integrate(0, lambda block: area_atm[:, lane_block(block)]), zeros, unroll=8
    )
    ones_up.wait_recv()
    ones_down.wait_recv()
    got_ocean = lax.fori_loop(
        0,
        margin,
        integrate(0, lambda block: ones_back[margin + block] + ones_low[block]),
        zeros,
        unroll=8,
    )
    got_ocean = lax.fori_loop(
        0,
        margin,
        integrate(margin, lambda block: ones_back[2 * margin + block] + ones_high[block]),
        got_ocean,
        unroll=8,
    )

    stacked = jnp.concatenate([target_ocean, got_ocean, target_atm, got_atm], axis=0)
    mine[...] = jnp.sum(jnp.transpose(stacked), axis=0, keepdims=True)

    def send_row(step, carry):
        pltpu.make_async_remote_copy(
            src_ref=mine,
            dst_ref=landed.at[step],
            send_sem=sum_send_sem,
            recv_sem=sum_recv_sem,
            device_id=partner(step),
            device_id_type=MESH,
        ).start()
        return carry

    pl.semaphore_wait(entered, layers - 1)
    lax.fori_loop(0, count - 1, send_row, 0)

    for copy in flux_sends[0] + flux_sends[1]:
        copy.wait_recv()
    lax.fori_loop(0, margin, spread(flux_low, 0), 0, unroll=8)
    lax.fori_loop(0, margin, spread(flux_high, margin + atm_span), 0, unroll=8)

    def forward(chunk, carry):
        for part in range(CHUNK):
            slot = chunk * CHUNK + part
            terms = jnp.dot(
                twice(flux_split[index[1, slot]]),
                jnp.concatenate([tiles_turned[slot, 0], tiles_turned[slot, 1]], axis=0),
                preferred_element_type=jnp.float32,
            )
            ocean_chain[slot + 1] = (
                terms[0:fields] + terms[fields : 2 * fields] + ocean_chain[index[2, slot]]
            )
        return carry

    lax.fori_loop(0, chunks, forward, 0)

    def place_ocean(block, carry):
        ocean_own[:, lane_block(block)] = ocean_chain[index[3, block]]
        return carry

    lax.fori_loop(0, ocean_span, place_ocean, 0, unroll=8)

    back_up.wait_recv()
    back_down.wait_recv()
    half = atm_cells - rim
    back_core[:, 0:rim] = (back_core[:, 0:rim] + got_low[...]) / area_atm[:, 0:rim]
    back_core[:, half:] = (back_core[:, half:] + got_high[...]) / area_atm[:, half:]

    pltpu.make_async_copy(landed, landed, sum_recv_sem).wait()
    sums = mine[...] + jnp.sum(landed[...], axis=0)
    columns = jnp.transpose(jnp.broadcast_to(sums, (LANES, LANES)))
    ratios[0] = columns[0:fields] / columns[fields : 2 * fields]
    ratios[1] = columns[2 * fields : 3 * fields] / columns[3 * fields :]
    for copy in (*flux_sends[0], *flux_sends[1], ones_up, ones_down, back_up, back_down):
        copy.wait_send()
    pltpu.make_async_copy(landed, landed, sum_send_sem).wait()


def scale_kernel(ocean, atm, ratios, ocean_out, atm_out, ocean_own, atm_own, store_sem):
    stores = []
    for part in range(ocean.shape[0] // 8):
        rows = pl.ds(part * 8, 8)
        for place, (source, own, target) in enumerate(
            ((ocean, ocean_own, ocean_out), (atm, atm_own, atm_out))
        ):
            ratio = ratios[place, rows, :]
            for block in range(source.shape[1] // LANES):
                cells = pl.ds(block * LANES, LANES)
                own[rows, cells] = source[rows, cells] * ratio
            stores.append(
                pltpu.make_async_copy(own.at[rows], target.at[rows], store_sem.at[part, place])
            )
            stores[-1].start()
    for store in stores:
        store.wait()


def on_device(atm_flux, ocean_state, area_atm, area_ocean, tiles, tile_row, tile_col, tile_count):
    fields, atm_cells = atm_flux.shape
    ocean_cells = ocean_state.shape[1]
    slots = tiles.shape[0]
    devices = lax.axis_size("curve")
    atm_span, ocean_span = atm_cells // LANES, ocean_cells // LANES
    margin = atm_span // 2
    window_span = atm_span + 2 * margin
    rim = margin * LANES
    f32, bf16 = jnp.float32, jnp.bfloat16
    hbm = pl.BlockSpec(memory_space=pltpu.HBM)
    vmem = pl.BlockSpec(memory_space=pltpu.VMEM)
    ocean_raw, atm_raw, ratios = pl.pallas_call(
        remap_kernel,
        out_shape=(
            pltpu.VMEM((fields, ocean_cells), f32),
            pltpu.VMEM((fields, atm_cells), f32),
            pltpu.VMEM((2, fields, LANES), f32),
        ),
        in_specs=[hbm] * 7 + [pl.BlockSpec(memory_space=pltpu.SMEM)],
        out_specs=(vmem, vmem, vmem),
        scratch_shapes=[
            pltpu.VMEM((1, atm_cells), f32),
            pltpu.VMEM((1, ocean_cells), f32),
            pltpu.VMEM((1, slots), jnp.int32),
            pltpu.VMEM((1, slots), jnp.int32),
            pltpu.VMEM((fields, atm_cells), f32),
            pltpu.VMEM((fields, rim), f32),
            pltpu.VMEM((fields, rim), f32),
            pltpu.VMEM((fields, ocean_cells), f32),
            pltpu.VMEM(tiles.shape, f32),
            pltpu.VMEM((slots, 2, LANES, LANES), bf16),
            pltpu.VMEM((ocean_span, 2 * fields + 16, LANES), bf16),
            pltpu.VMEM((window_span, 2 * fields, LANES), bf16),
            pltpu.VMEM((slots + 1, fields + 8, LANES), f32),
            pltpu.VMEM((slots + 1, fields, LANES), f32),
            pltpu.VMEM((fields, rim), f32),
            pltpu.VMEM((fields, rim), f32),
            pltpu.VMEM((fields, rim), f32),
            pltpu.VMEM((fields, rim), f32),
            pltpu.VMEM((window_span, 1, LANES), f32),
            pltpu.VMEM((margin, 1, LANES), f32),
            pltpu.VMEM((margin, 1, LANES), f32),
            pltpu.VMEM((8, LANES), jnp.int32),
            pltpu.SMEM((8, LANES), jnp.int32),
            pltpu.VMEM((1, LANES), f32),
            pltpu.VMEM((devices - 1, 1, LANES), f32),
            pltpu.SemaphoreType.REGULAR,
            pltpu.SemaphoreType.DMA((6,)),
            pltpu.SemaphoreType.DMA((slots // CHUNK,)),
            pltpu.SemaphoreType.DMA,
            pltpu.SemaphoreType.DMA((4,)),
            pltpu.SemaphoreType.DMA((4,)),
            pltpu.SemaphoreType.DMA((2,)),
            pltpu.SemaphoreType.DMA((2,)),
            pltpu.SemaphoreType.DMA((2,)),
            pltpu.SemaphoreType.DMA((2,)),
            pltpu.SemaphoreType.DMA,
            pltpu.SemaphoreType.DMA,
        ],
        compiler_params=pltpu.CompilerParams(
            collective_id=0, has_side_effects=True, vmem_limit_bytes=40 * MIB
        ),
        name="remap",
    )(
        *(
            pltpu.with_memory_space_constraint(operand, pltpu.HBM)
            for operand in (
                atm_flux,
                ocean_state,
                area_atm.reshape(1, atm_cells),
                area_ocean.reshape(1, ocean_cells),
                tiles,
                tile_row.reshape(1, slots),
                tile_col.reshape(1, slots),
            )
        ),
        tile_count,
    )
    return pl.pallas_call(
        scale_kernel,
        out_shape=(
            jax.ShapeDtypeStruct((fields, ocean_cells), f32),
            jax.ShapeDtypeStruct((fields, atm_cells), f32),
        ),
        in_specs=[vmem] * 3,
        out_specs=(hbm, hbm),
        scratch_shapes=[
            pltpu.VMEM((fields, ocean_cells), f32),
            pltpu.VMEM((fields, atm_cells), f32),
            pltpu.SemaphoreType.DMA((fields // 8, 2)),
        ],
        compiler_params=pltpu.CompilerParams(vmem_limit_bytes=8 * MIB),
        name="scale",
    )(ocean_raw, atm_raw, ratios)


def solution(mesh):
    in_specs = (
        P("field", "curve"),
        P("field", "curve"),
        P("curve"),
        P("curve"),
        P("curve", None, None),
        P("curve"),
        P("curve"),
        P("curve"),
    )
    out_specs = (P("field", "curve"), P("field", "curve"))
    return jax.shard_map(
        on_device, mesh=mesh, in_specs=in_specs, out_specs=out_specs, check_vma=False
    )
```

```python
import functools

import jax
import jax.numpy as jnp
from jax import lax
from jax.experimental import pallas as pl
from jax.experimental.pallas import tpu as pltpu
from jax.sharding import PartitionSpec as P

MESH = pl.DeviceIdType.MESH
LANES = 128
PLANE = 16
CHUNK = 32
MIB = 1024 * 1024


def split(values):
    high = values.astype(jnp.bfloat16)
    return high, (values - high.astype(jnp.float32)).astype(jnp.bfloat16)


def twice(block):
    return jnp.concatenate([block, block], axis=1)


def lane_block(index):
    return pl.ds(pl.multiple_of(index * LANES, LANES), LANES)


def remap_kernel(
    flux,
    state,
    area_atm_in,
    area_ocean_in,
    tiles,
    tile_row_in,
    tile_col_in,
    tile_count,
    ocean_own,
    back_core,
    ratios,
    area_atm,
    area_ocean,
    tile_row,
    tile_col,
    flux_own,
    flux_low,
    flux_high,
    state_own,
    tiles_own,
    tiles_turned,
    state_split,
    flux_split,
    back_chain,
    ocean_chain,
    send_low,
    send_high,
    got_low,
    got_high,
    ones_back,
    ones_low,
    ones_high,
    table,
    index,
    mine,
    landed,
    entered,
    load_sem,
    tile_sem,
    index_sem,
    flux_send_sem,
    flux_recv_sem,
    ones_send_sem,
    ones_recv_sem,
    back_send_sem,
    back_recv_sem,
    sum_send_sem,
    sum_recv_sem,
):
    count = lax.axis_size("curve")
    me = lax.axis_index("curve")
    core = lax.axis_index("field")
    above = (lax.rem(me + 1, count), core)
    below = (lax.rem(me + count - 1, count), core)
    fields, atm_cells = flux.shape
    ocean_cells = state.shape[1]
    slots = tiles.shape[0]
    atm_span, ocean_span = atm_cells // LANES, ocean_cells // LANES
    margin = atm_span // 2
    window_span = atm_span + 2 * margin
    rim = margin * LANES

    layers = count // PLANE
    layer, place = me // PLANE, me % PLANE

    def partner(away):
        return (lax.bitwise_and(me + away, count - 1), core)

    def plane_partner(step):
        return (layer * PLANE + lax.bitwise_and(place + step, PLANE - 1), core)

    def line_partner(step):
        return (lax.bitwise_and(layer + step, layers - 1) * PLANE + place, core)

    barrier = pltpu.get_barrier_semaphore()

    def greet(semaphore, partner_of, partners):
        for step in range(1, partners):
            pl.semaphore_signal(semaphore, inc=1, device_id=partner_of(step), device_id_type=MESH)

    for neighbour in (above, below):
        pl.semaphore_signal(barrier, inc=1, device_id=neighbour, device_id_type=MESH)
    greet(barrier, line_partner, layers)
    greet(barrier, plane_partner, PLANE)

    loads = [
        pltpu.make_async_copy(source, target, load_sem.at[place])
        for place, (source, target) in enumerate(
            (
                (tile_row_in, tile_row),
                (tile_col_in, tile_col),
                (area_ocean_in, area_ocean),
                (state, state_own),
                (area_atm_in, area_atm),
                (flux, flux_own),
            )
        )
    ]
    for load in loads[0:4]:
        load.start()
    chunks = slots // CHUNK

    def load_tiles(chunk):
        part = pl.ds(chunk * CHUNK, CHUNK)
        return pltpu.make_async_copy(tiles.at[part], tiles_own.at[part], tile_sem.at[chunk])

    for chunk in range(chunks):
        load_tiles(chunk).start()
    for load in loads[4:6]:
        load.start()

    for load in loads[0:2]:
        load.wait()
    slot_of_row = lax.broadcasted_iota(jnp.int32, (slots, LANES), 0)
    lane = lax.broadcasted_iota(jnp.int32, (slots, LANES), 1)
    live = slot_of_row < tile_count[0]

    def chain_of(names):
        across = jnp.broadcast_to(names, (slots, LANES))
        down = jnp.transpose(across.astype(jnp.float32)).astype(jnp.int32)
        former = jnp.where((across == down) & (slot_of_row < lane), slot_of_row + 1, 0)
        last = jnp.where((lane == down) & live, slot_of_row + 1, 0)
        return jnp.max(former, axis=0, keepdims=True), jnp.max(last, axis=0, keepdims=True)

    row_names = tile_row[...] - me * ocean_span
    col_names = tile_col[...] - me * atm_span + margin
    ring = atm_span * count
    col_names = jnp.where(col_names < 0, col_names + ring, col_names)
    col_names = jnp.where(col_names >= ring, col_names - ring, col_names)
    row_names = jnp.clip(row_names, 0, ocean_span - 1)
    col_names = jnp.clip(col_names, 0, window_span - 1)
    row_former, row_last = chain_of(row_names)
    col_former, col_last = chain_of(col_names)
    for line, row in enumerate(
        (row_names, col_names, row_former, row_last, col_former, col_last)
    ):
        table[line : line + 1, :] = row
    table[6:8, :] = jnp.zeros((2, LANES), jnp.int32)
    index_copy = pltpu.make_async_copy(table, index, index_sem)
    index_copy.start()

    def remote(source, target, sends, receives, place, device):
        return pltpu.make_async_remote_copy(
            src_ref=source,
            dst_ref=target,
            send_sem=sends.at[place],
            recv_sem=receives.at[place],
            device_id=device,
            device_id_type=MESH,
        )

    pl.semaphore_wait(barrier, PLANE + layers)
    greet(entered, line_partner, layers)

    half_fields = fields // 2
    flux_sends = []
    for half in range(2):
        rows = pl.ds(half * half_fields, half_fields)
        flux_sends.append(
            (
                remote(
                    flux.at[rows, pl.ds(atm_cells - rim, rim)],
                    flux_low.at[rows],
                    flux_send_sem,
                    flux_recv_sem,
                    2 * half,
                    above,
                ),
                remote(
                    flux.at[rows, pl.ds(0, rim)],
                    flux_high.at[rows],
                    flux_send_sem,
                    flux_recv_sem,
                    2 * half + 1,
                    below,
                ),
            )
        )
    for copy in flux_sends[0]:
        copy.start()

    zeros = jnp.zeros((fields, LANES), jnp.float32)
    extra = lax.broadcasted_iota(jnp.int32, (16, LANES), 0)
    for load in loads[2:4]:
        load.wait()

    def weigh(block, acc):
        area = area_ocean[:, lane_block(block)]
        weighted = state_own[:, lane_block(block)] * area
        high, low = split(weighted)
        state_split[block, 0:fields, :] = high
        state_split[block, fields : 2 * fields, :] = low
        area_high = area.astype(jnp.bfloat16).astype(jnp.float32)
        area_rows = jnp.where(
            extra == 0, area_high, jnp.where(extra == 1, area - area_high, 0.0)
        )
        state_split[block, 2 * fields : 2 * fields + 16, :] = area_rows.astype(jnp.bfloat16)
        return acc + weighted

    target_atm = lax.fori_loop(0, ocean_span, weigh, zeros, unroll=8)

    back_chain[0] = jnp.zeros(back_chain.shape[1:], jnp.float32)
    ocean_chain[0] = jnp.zeros(ocean_chain.shape[1:], jnp.float32)
    index_copy.wait()

    def backward(chunk, carry):
        load_tiles(chunk).wait()
        for part in range(CHUNK):
            slot = chunk * CHUNK + part
            weights = tiles_own[slot]
            high, low = split(weights.T)
            tiles_turned[slot, 0] = high
            tiles_turned[slot, 1] = low
            terms = jnp.dot(
                twice(state_split[index[0, slot]]),
                jnp.concatenate(split(weights), axis=0),
                preferred_element_type=jnp.float32,
            )
            former = index[4, slot]
            back_chain[slot + 1, 0:fields, :] = (
                terms[0:fields] + terms[fields : 2 * fields] + back_chain[former, 0:fields, :]
            )
            back_chain[slot + 1, fields : fields + 8, :] = (
                terms[2 * fields : 2 * fields + 8] + back_chain[former, fields : fields + 8, :]
            )
        return carry

    lax.fori_loop(0, chunks, backward, 0)

    def collect(target, first):
        def one(block, acc):
            slot = index[5, first + block]
            sums = back_chain[slot, 0:fields, :]
            target[:, lane_block(block)] = sums
            ones_back[first + block] = jnp.sum(
                back_chain[slot, fields : fields + 8, :], axis=0, keepdims=True
            )
            return acc + sums

        return one

    got_atm = lax.fori_loop(0, margin, collect(send_low, 0), zeros, unroll=8)
    ones_down = remote(
        ones_back.at[pl.ds(0, margin)], ones_high, ones_send_sem, ones_recv_sem, 1, below
    )
    ones_down.start()
    got_atm = lax.fori_loop(0, margin, collect(send_high, margin + atm_span), got_atm, unroll=8)
    ones_up = remote(
        ones_back.at[pl.ds(margin + atm_span, margin)],
        ones_low,
        ones_send_sem,
        ones_recv_sem,
        0,
        above,
    )
    ones_up.start()
    for copy in flux_sends[1]:
        copy.start()
    back_down = remote(send_low, got_high, back_send_sem, back_recv_sem, 1, below)
    back_up = remote(send_high, got_low, back_send_sem, back_recv_sem, 0, above)
    back_down.start()
    back_up.start()
    got_atm = lax.fori_loop(0, atm_span, collect(back_core, margin), got_atm, unroll=8)

    for load in loads[4:6]:
        load.wait()

    def spread(source, first):
        def one(block, carry):
            high, low = split(source[:, lane_block(block)])
            flux_split[first + block, 0:fields, :] = high
            flux_split[first + block, fields : 2 * fields, :] = low
            return carry

        return one

    def integrate(first, factors):
        def one(block, acc):
            return acc + flux_own[:, lane_block(first + block)] * factors(block)

        return one

    lax.fori_loop(0, atm_span, spread(flux_own, margin), 0, unroll=8)
    target_ocean = lax.fori_loop(
        0, atm_span, integrate(0, lambda block: area_atm[:, lane_block(block)]), zeros, unroll=8
    )
    ones_up.wait_recv()
    ones_down.wait_recv()
    got_ocean = lax.fori_loop(
        0,
        margin,
        integrate(0, lambda block: ones_back[margin + block] + ones_low[block]),
        zeros,
        unroll=8,
    )
    got_ocean = lax.fori_loop(
        0,
        margin,
        integrate(margin, lambda block: ones_back[2 * margin + block] + ones_high[block]),
        got_ocean,
        unroll=8,
    )

    stacked = jnp.concatenate([target_ocean, got_ocean, target_atm, got_atm], axis=0)
    mine[...] = jnp.sum(jnp.transpose(stacked), axis=0, keepdims=True)

    def send_row(away, slot):
        pltpu.make_async_remote_copy(
            src_ref=mine,
            dst_ref=landed.at[slot],
            send_sem=sum_send_sem,
            recv_sem=sum_recv_sem,
            device_id=partner(away),
            device_id_type=MESH,
        ).start()

    def send_pair(step, carry):
        send_row(count // 2 + step, 2 * step)
        send_row(count // 2 - step, 2 * step - 1)
        return carry

    pl.semaphore_wait(entered, layers - 1)
    send_row(count // 2, 0)
    lax.fori_loop(1, count // 2, send_pair, 0, unroll=3)

    for copy in flux_sends[0] + flux_sends[1]:
        copy.wait_recv()
    lax.fori_loop(0, margin, spread(flux_low, 0), 0, unroll=8)
    lax.fori_loop(0, margin, spread(flux_high, margin + atm_span), 0, unroll=8)

    def forward(chunk, carry):
        for part in range(CHUNK):
            slot = chunk * CHUNK + part
            terms = jnp.dot(
                twice(flux_split[index[1, slot]]),
                jnp.concatenate([tiles_turned[slot, 0], tiles_turned[slot, 1]], axis=0),
                preferred_element_type=jnp.float32,
            )
            ocean_chain[slot + 1] = (
                terms[0:fields] + terms[fields : 2 * fields] + ocean_chain[index[2, slot]]
            )
        return carry

    lax.fori_loop(0, chunks, forward, 0)

    def place_ocean(block, carry):
        ocean_own[:, lane_block(block)] = ocean_chain[index[3, block]]
        return carry

    lax.fori_loop(0, ocean_span, place_ocean, 0, unroll=8)

    back_up.wait_recv()
    back_down.wait_recv()
    half = atm_cells - rim
    back_core[:, 0:rim] = (back_core[:, 0:rim] + got_low[...]) / area_atm[:, 0:rim]
    back_core[:, half:] = (back_core[:, half:] + got_high[...]) / area_atm[:, half:]

    pltpu.make_async_copy(landed, landed, sum_recv_sem).wait()
    sums = mine[...] + jnp.sum(landed[...], axis=0)
    columns = jnp.transpose(jnp.broadcast_to(sums, (LANES, LANES)))
    ratios[0] = columns[0:fields] / columns[fields : 2 * fields]
    ratios[1] = columns[2 * fields : 3 * fields] / columns[3 * fields :]
    for copy in (*flux_sends[0], *flux_sends[1], ones_up, ones_down, back_up, back_down):
        copy.wait_send()
    pltpu.make_async_copy(landed, landed, sum_send_sem).wait()


def scale_kernel(ocean, atm, ratios, ocean_out, atm_out, ocean_own, atm_own, store_sem):
    stores = []
    for part in range(ocean.shape[0] // 8):
        rows = pl.ds(part * 8, 8)
        for place, (source, own, target) in enumerate(
            ((ocean, ocean_own, ocean_out), (atm, atm_own, atm_out))
        ):
            ratio = ratios[place, rows, :]
            for block in range(source.shape[1] // LANES):
                cells = pl.ds(block * LANES, LANES)
                own[rows, cells] = source[rows, cells] * ratio
            stores.append(
                pltpu.make_async_copy(own.at[rows], target.at[rows], store_sem.at[part, place])
            )
            stores[-1].start()
    for store in stores:
        store.wait()


def on_device(atm_flux, ocean_state, area_atm, area_ocean, tiles, tile_row, tile_col, tile_count):
    fields, atm_cells = atm_flux.shape
    ocean_cells = ocean_state.shape[1]
    slots = tiles.shape[0]
    devices = lax.axis_size("curve")
    atm_span, ocean_span = atm_cells // LANES, ocean_cells // LANES
    margin = atm_span // 2
    window_span = atm_span + 2 * margin
    rim = margin * LANES
    f32, bf16 = jnp.float32, jnp.bfloat16
    hbm = pl.BlockSpec(memory_space=pltpu.HBM)
    vmem = pl.BlockSpec(memory_space=pltpu.VMEM)
    ocean_raw, atm_raw, ratios = pl.pallas_call(
        remap_kernel,
        out_shape=(
            pltpu.VMEM((fields, ocean_cells), f32),
            pltpu.VMEM((fields, atm_cells), f32),
            pltpu.VMEM((2, fields, LANES), f32),
        ),
        in_specs=[hbm] * 7 + [pl.BlockSpec(memory_space=pltpu.SMEM)],
        out_specs=(vmem, vmem, vmem),
        scratch_shapes=[
            pltpu.VMEM((1, atm_cells), f32),
            pltpu.VMEM((1, ocean_cells), f32),
            pltpu.VMEM((1, slots), jnp.int32),
            pltpu.VMEM((1, slots), jnp.int32),
            pltpu.VMEM((fields, atm_cells), f32),
            pltpu.VMEM((fields, rim), f32),
            pltpu.VMEM((fields, rim), f32),
            pltpu.VMEM((fields, ocean_cells), f32),
            pltpu.VMEM(tiles.shape, f32),
            pltpu.VMEM((slots, 2, LANES, LANES), bf16),
            pltpu.VMEM((ocean_span, 2 * fields + 16, LANES), bf16),
            pltpu.VMEM((window_span, 2 * fields, LANES), bf16),
            pltpu.VMEM((slots + 1, fields + 8, LANES), f32),
            pltpu.VMEM((slots + 1, fields, LANES), f32),
            pltpu.VMEM((fields, rim), f32),
            pltpu.VMEM((fields, rim), f32),
            pltpu.VMEM((fields, rim), f32),
            pltpu.VMEM((fields, rim), f32),
            pltpu.VMEM((window_span, 1, LANES), f32),
            pltpu.VMEM((margin, 1, LANES), f32),
            pltpu.VMEM((margin, 1, LANES), f32),
            pltpu.VMEM((8, LANES), jnp.int32),
            pltpu.SMEM((8, LANES), jnp.int32),
            pltpu.VMEM((1, LANES), f32),
            pltpu.VMEM((devices - 1, 1, LANES), f32),
            pltpu.SemaphoreType.REGULAR,
            pltpu.SemaphoreType.DMA((6,)),
            pltpu.SemaphoreType.DMA((slots // CHUNK,)),
            pltpu.SemaphoreType.DMA,
            pltpu.SemaphoreType.DMA((4,)),
            pltpu.SemaphoreType.DMA((4,)),
            pltpu.SemaphoreType.DMA((2,)),
            pltpu.SemaphoreType.DMA((2,)),
            pltpu.SemaphoreType.DMA((2,)),
            pltpu.SemaphoreType.DMA((2,)),
            pltpu.SemaphoreType.DMA,
            pltpu.SemaphoreType.DMA,
        ],
        compiler_params=pltpu.CompilerParams(
            collective_id=0, has_side_effects=True, vmem_limit_bytes=40 * MIB
        ),
        name="remap",
    )(
        *(
            pltpu.with_memory_space_constraint(operand, pltpu.HBM)
            for operand in (
                atm_flux,
                ocean_state,
                area_atm.reshape(1, atm_cells),
                area_ocean.reshape(1, ocean_cells),
                tiles,
                tile_row.reshape(1, slots),
                tile_col.reshape(1, slots),
            )
        ),
        tile_count,
    )
    return pl.pallas_call(
        scale_kernel,
        out_shape=(
            jax.ShapeDtypeStruct((fields, ocean_cells), f32),
            jax.ShapeDtypeStruct((fields, atm_cells), f32),
        ),
        in_specs=[vmem] * 3,
        out_specs=(hbm, hbm),
        scratch_shapes=[
            pltpu.VMEM((fields, ocean_cells), f32),
            pltpu.VMEM((fields, atm_cells), f32),
            pltpu.SemaphoreType.DMA((fields // 8, 2)),
        ],
        compiler_params=pltpu.CompilerParams(vmem_limit_bytes=8 * MIB),
        name="scale",
    )(ocean_raw, atm_raw, ratios)


def solution(mesh):
    in_specs = (
        P("field", "curve"),
        P("field", "curve"),
        P("curve"),
        P("curve"),
        P("curve", None, None),
        P("curve"),
        P("curve"),
        P("curve"),
    )
    out_specs = (P("field", "curve"), P("field", "curve"))
    return jax.shard_map(
        on_device, mesh=mesh, in_specs=in_specs, out_specs=out_specs, check_vma=False
    )
```
